128 devices in a mesh: dp: 2 (over x_hi), mp: 64 (over y, x_lo, z, core).
Axes of the slice: x: 4 (x_hi: 2, x_lo: 2; x = x_hi * 2 + x_lo), y: 4, z: 4, core: 2. Of those that a mesh axis runs over, the one named last changes fastest.
Arguments:
- activations: bfloat16 [4096, 8192], P('dp', 'mp'), may hold values from -6 to 6
- w_up: bfloat16 [5, 128, 32768], P(None, None, 'mp'), may hold values from -0.25 to 0.25
- w_down: bfloat16 [5, 32768, 128], P(None, 'mp'), may hold values from -0.125 to 0.125
- u_up: bfloat16 [8192, 128], P('mp'), may hold values from -0.0625 to 0.0625
- v_up: bfloat16 [128, 32768], P(None, 'mp'), may hold values from -0.5 to 0.5
- u_down: bfloat16 [32768, 128], P('mp'), may hold values from -0.03125 to 0.03125
- v_down: bfloat16 [128, 8192], P(None, 'mp'), may hold values from -0.5 to 0.5
- mask_up: int32 [4, 64], P(None, 'mp'), may hold values 0 or 1
- mask_down: int32 [4, 64], P(None, 'mp'), may hold values 0 or 1
- grad_y: bfloat16 [4096, 8192], P('dp', 'mp'), may hold values from -6 to 6
Outputs:
- output: bfloat16 [4096, 8192], P('dp', 'mp')
- grad_x: bfloat16 [4096, 8192], P('dp', 'mp')
- grad_w_up: float32 [5, 128, 32768], P(None, None, 'mp')
- grad_w_down: float32 [5, 32768, 128], P(None, 'mp')
- grad_u_up: float32 [8192, 128], P('mp')
- grad_v_up: float32 [128, 32768], P(None, 'mp')
- grad_u_down: float32 [32768, 128], P('mp')
- grad_v_down: float32 [128, 8192], P(None, 'mp')
The draws below stay inside these ranges and needn't reach their ends.
All inputs are finite; a program needn't handle non-finite values. No bound on the sum of `mask_up` or of `mask_down` on one device may be relied on, other than what follows from the above.
Results may differ from the reference program's by a relative error of at most 0.008.
Values may be sent and summed in bfloat16 or wider, within the bound.
No kernel may reach another device: no remote copies, remote signals or barrier semaphores. Data moves between devices by JAX's collectives and lax.ppermute only.
A program may use at most 128 MiB of HBM per device.

```python
import jax
import jax.numpy as jnp

D = 8192
FF = 32768
RANK = 128
LEVELS = 4
TOKENS = 4096
DG = 128
HG = 512
N_MP = 64


def touch_ends(drawn, stream_key, low, largest):
    index_at = [jax.random.randint(jax.random.fold_in(stream_key, axis), (), 0, length) for axis, length in enumerate(drawn.shape)]
    main_axis = drawn.shape.index(max(drawn.shape))
    next_to = index_at[:main_axis] + [(index_at[main_axis] + 1) % drawn.shape[main_axis]] + index_at[main_axis + 1:]
    return drawn.at[tuple(index_at)].set(low).at[tuple(next_to)].set(largest)


def level_of(stream_key, dims, pieces, low, top_value):
    def one(axis_at, shards_of):
        heights = jax.random.uniform(jax.random.fold_in(jax.random.fold_in(stream_key, 6), axis_at), (shards_of,), jnp.float32, low / len(pieces), top_value / len(pieces))
        return jnp.repeat(jnp.exp(heights), dims[axis_at] // shards_of).reshape((-1,) + (1,) * (len(dims) - axis_at - 1))

    gain = one(*pieces[0])
    for cut in pieces[1:]:
        gain = gain * one(*cut)
    return gain


def gaussian(rng, shape, deviation, limit, shards=(), held_as=jnp.bfloat16):
    drawn = jax.random.normal(rng, shape, jnp.float32) * deviation
    if len(shards) > 0:
        drawn = level_of(rng, shape, shards, -0.22, 0.18) * drawn
    return jnp.clip(drawn, min=-limit, max=limit).astype(held_as)


def setup_inputs(seed: int = 0) -> dict:
    splits = jax.random.split(jax.random.key(seed), 11)
    activations = gaussian(splits[0], (TOKENS, D), 1.0, 6.0, ((0, 2), (1, 64)))
    w_up = gaussian(splits[1], (LEVELS + 1, DG, FF), ((LEVELS + 1) * DG) ** -0.5, 0.25, ((2, 64),))
    w_down = gaussian(splits[2], (LEVELS + 1, FF, DG), ((LEVELS + 1) * HG) ** -0.5, 0.125, ((1, 64),))
    u_up = gaussian(splits[3], (D, RANK), D ** -0.5, 0.0625, ((0, 64),))
    v_up = gaussian(splits[4], (RANK, FF), RANK ** -0.5, 0.5, ((1, 64),))
    u_down = gaussian(splits[5], (FF, RANK), FF ** -0.5, 0.03125, ((0, 64),))
    v_down = gaussian(splits[6], (RANK, D), RANK ** -0.5, 0.5, ((1, 64),))
    mask_up = touch_ends((jax.random.randint(splits[7], (LEVELS, N_MP), 0, 4) < 3).astype(jnp.int32), jax.random.fold_in(splits[7], 1), 0, 1)
    mask_down = touch_ends((jax.random.randint(splits[8], (LEVELS, N_MP), 0, 4) < 3).astype(jnp.int32), jax.random.fold_in(splits[8], 1), 0, 1)
    grad_y = gaussian(splits[9], (TOKENS, D), 1.0, 6.0, ((0, 2), (1, 64)))
    return {"activations": activations, "w_up": w_up, "w_down": w_down, "u_up": u_up, "v_up": v_up, "u_down": u_down, "v_down": v_down, "mask_up": mask_up, "mask_down": mask_down, "grad_y": grad_y}


def gelu_tanh(value):
    return jax.nn.gelu(value, approximate=True)

def reference(activations, w_up, w_down, u_up, v_up, u_down, v_down, mask_up, mask_down, grad_y):
    f32 = jnp.float32
    groups = jnp.arange(N_MP, dtype=jnp.int32)
    x_blocks = activations.astype(f32).reshape(TOKENS, N_MP, DG)
    wu_blocks = w_up.astype(f32).reshape(LEVELS + 1, DG, N_MP, HG)
    wd_blocks = w_down.astype(f32).reshape(LEVELS + 1, N_MP, HG, DG)
    mu_float = mask_up.astype(f32)
    md_float = mask_down.astype(f32)
    z_up = jnp.dot(activations, u_up, preferred_element_type=f32).astype(jnp.bfloat16)
    pre = jnp.einsum('tgd,dgh->tgh', x_blocks, wu_blocks[0])
    for level in range(LEVELS):
        partner = jnp.bitwise_xor(groups, jnp.int32(1 << level))
        term = jnp.einsum('tgd,dgh->tgh', x_blocks[:, partner], wu_blocks[level + 1])
        pre = pre + term * mu_float[level][None, :, None]
    pre = pre.reshape(TOKENS, FF) + jnp.dot(z_up, v_up, preferred_element_type=f32)
    hidden = gelu_tanh(pre).astype(jnp.bfloat16)
    hid_blocks = hidden.astype(f32).reshape(TOKENS, N_MP, HG)
    z_down = jnp.dot(hidden, u_down, preferred_element_type=f32).astype(jnp.bfloat16)
    out = jnp.einsum('tgh,ghd->tgd', hid_blocks, wd_blocks[0])
    for level in range(LEVELS):
        partner = jnp.bitwise_xor(groups, jnp.int32(1 << level))
        term = jnp.einsum('tgh,ghd->tgd', hid_blocks[:, partner], wd_blocks[level + 1][partner])
        out = out + term * md_float[level][None, :, None]
    output = (out.reshape(TOKENS, D) + jnp.dot(z_down, v_down, preferred_element_type=f32)).astype(jnp.bfloat16)
    gy_blocks = grad_y.astype(f32).reshape(TOKENS, N_MP, DG)
    grad_v_down = jnp.dot(z_down.T, grad_y, preferred_element_type=f32)
    gz_down = jnp.dot(grad_y, v_down.T, preferred_element_type=f32).astype(jnp.bfloat16)
    grad_u_down = jnp.dot(hidden.T, gz_down, preferred_element_type=f32)
    gwd_list = [jnp.einsum('tgh,tgd->ghd', hid_blocks, gy_blocks)]
    grad_hid = jnp.einsum('tgd,ghd->tgh', gy_blocks, wd_blocks[0])
    for level in range(LEVELS):
        partner = jnp.bitwise_xor(groups, jnp.int32(1 << level))
        masked = gy_blocks[:, partner] * md_float[level][partner][None, :, None]
        gwd_list.append(jnp.einsum('tgh,tgd->ghd', hid_blocks, masked))
        grad_hid = grad_hid + jnp.einsum('tgd,ghd->tgh', masked, wd_blocks[level + 1])
    grad_w_down = jnp.stack(gwd_list).reshape(LEVELS + 1, FF, DG)
    grad_hid = grad_hid.reshape(TOKENS, FF) + jnp.dot(gz_down, u_down.T, preferred_element_type=f32)
    unused, pullback = jax.vjp(gelu_tanh, pre)
    grad_pre = pullback(grad_hid)[0].astype(jnp.bfloat16)
    grad_v_up = jnp.dot(z_up.T, grad_pre, preferred_element_type=f32)
    gz_up = jnp.dot(grad_pre, v_up.T, preferred_element_type=f32).astype(jnp.bfloat16)
    grad_u_up = jnp.dot(activations.T, gz_up, preferred_element_type=f32)
    gp_blocks = grad_pre.astype(f32).reshape(TOKENS, N_MP, HG)
    gwu_list = [jnp.einsum('tgd,tgh->dgh', x_blocks, gp_blocks)]
    grad_in = jnp.einsum('tgh,dgh->tgd', gp_blocks, wu_blocks[0])
    for level in range(LEVELS):
        partner = jnp.bitwise_xor(groups, jnp.int32(1 << level))
        gwu_list.append(jnp.einsum('tgd,tgh->dgh', x_blocks[:, partner], gp_blocks) * mu_float[level][None, :, None])
        masked = gp_blocks * mu_float[level][None, :, None]
        term = jnp.einsum('tgh,dgh->tgd', masked, wu_blocks[level + 1])
        grad_in = grad_in + term[:, partner]
    grad_w_up = jnp.stack(gwu_list).reshape(LEVELS + 1, DG, FF)
    grad_x = (grad_in.reshape(TOKENS, D) + jnp.dot(gz_up, u_up.T, preferred_element_type=f32)).astype(jnp.bfloat16)
    return (output, grad_x, grad_w_up, grad_w_down, grad_u_up, grad_v_up, grad_u_down, grad_v_down)
```

```python
import jax
import jax.numpy as jnp
from jax import lax
from jax.experimental import pallas as pl
from jax.experimental.pallas import tpu as pltpu
from jax.sharding import PartitionSpec as P

BF = jnp.bfloat16
F32 = jnp.float32
LEVEL_AXES = (("c", 1), ("z", 1), ("z", 2), ("xl", 1))
CHIPS = ("y", "xl", "z")
PAD = 16
TILE = 512
GELU_C = 0.7978845608028654
GELU_A = 0.044715


def swapped(array, axis, bit):
    return lax.ppermute(array, axis, [(i, i ^ bit) for i in range(lax.axis_size(axis))])


def matmul(left, right):
    return jnp.dot(left, right, preferred_element_type=F32)


def matmul_nt(left, right):
    return lax.dot_general(left, right, (((1,), (1,)), ((), ())), preferred_element_type=F32)


def matmul_tn(left, right):
    return lax.dot_general(left, right, (((0,), (0,)), ((), ())), preferred_element_type=F32)


def sum_over_mp(part):
    rows, width = part.shape
    half = rows // 2
    chips = lax.axis_size("y") * lax.axis_size("xl") * lax.axis_size("z")
    core = lax.axis_index("c")
    mine = lax.dynamic_slice_in_dim(part, core * half, half, 0)
    other = lax.dynamic_slice_in_dim(part, (1 - core) * half, half, 0)
    got = swapped(other, "c", 1)
    both = (mine.astype(F32) + got.astype(F32)).astype(BF)
    split = lax.all_to_all(both.reshape(chips, half // chips, width), CHIPS, 0, 0, tiled=False)
    total = jnp.sum(split.astype(F32), axis=0).astype(BF)
    spread = jnp.broadcast_to(total[None], (chips,) + total.shape)
    whole = lax.all_to_all(spread, CHIPS, 0, 0, tiled=False).reshape(half, width)
    away = swapped(whole, "c", 1)
    low = jnp.where(core == 0, whole, away)
    high = jnp.where(core == 0, away, whole)
    return jnp.concatenate([low, high], axis=0)


def mid_kernel(mu_ref, xg_ref, r0, r1, r2, r3, k0, k1, k2, k3, z_ref, wu_ref, vu_ref, wd_ref, ud_ref,
               hid_ref, gp_ref, own_ref, s0, s1, s2, s3, part_ref, wu6, wd6, wdm6):
    sends = (s0, s1, s2, s3)

    @pl.when(pl.program_id(0) == 0)
    def _():
        wu6[0:128, :] = wu_ref[0]
        wd6[:, 0:128] = wd_ref[0]
        wdm6[:, 0:128] = wd_ref[0]
        for k, mask_rows in enumerate((k0, k1, k2, k3)):
            lo = 128 * (k + 1)
            wu6[lo:lo + 128, :] = (wu_ref[k + 1].astype(F32) * mu_ref[k]).astype(BF)
            wd6[:, lo:lo + 128] = wd_ref[k + 1]
            wdm6[:, lo:lo + 128] = (wd_ref[k + 1].astype(F32) * mask_rows[k:k + 1, 0:128].astype(F32)).astype(BF)
        wu6[640:768, :] = vu_ref[...]
        wd6[:, 640:768] = ud_ref[...]
        wdm6[:, 640:768] = ud_ref[...]

    refs = (xg_ref, r0, r1, r2, r3, z_ref)
    x6 = jnp.concatenate([r[:, 0:128] for r in refs], axis=1)
    gy6 = jnp.concatenate([r[:, 128:256] for r in refs], axis=1)
    pre = matmul(x6, wu6[...])
    square = pre * pre
    tanh = jnp.tanh(GELU_C * pre * (1.0 + GELU_A * square))
    cdf = 0.5 * (1.0 + tanh)
    hidden = (pre * cdf).astype(BF)
    hid_ref[...] = hidden
    slope = cdf + (0.5 * GELU_C) * pre * (1.0 - tanh * tanh) * (1.0 + (3.0 * GELU_A) * square)
    grad_hid = matmul_nt(gy6, wdm6[...])
    grad_pre = (grad_hid * slope).astype(BF)
    gp_ref[...] = grad_pre
    down = matmul(hidden, wd6[...])
    back = matmul_nt(grad_pre, wu6[...])
    own_ref[:, 0:128] = down[:, 0:128]
    own_ref[:, 128:256] = back[:, 0:128]
    for k, send in enumerate(sends):
        lo = 128 * (k + 1)
        send[:, 0:128] = down[:, lo:lo + 128].astype(BF)
        send[:, 128:256] = back[:, lo:lo + 128].astype(BF)
    part_ref[:, 0:128] = down[:, 640:768].astype(BF)
    part_ref[:, 128:256] = back[:, 640:768].astype(BF)


def mid(mu, xg, recv, z, w_up, v_up, w_down, u_down):
    tokens = z.shape[0]
    hg = w_up.shape[2]
    row = lambda width: pl.BlockSpec((TILE, width), lambda i: (i, 0))
    full = lambda a: pl.BlockSpec(a.shape, lambda i, n=a.ndim: (0,) * n)
    mask_rows = pl.BlockSpec((PAD, 256), lambda i: (tokens // PAD, 0))
    sds = jax.ShapeDtypeStruct
    return pl.pallas_call(
        mid_kernel,
        grid=(tokens // TILE,),
        in_specs=[pl.BlockSpec(memory_space=pltpu.SMEM)] + [row(256)] * 5 + [mask_rows] * 4 + [row(256)]
        + [full(w_up), full(v_up), full(w_down), full(u_down)],
        out_specs=[row(hg), row(hg), row(256)] + [row(256)] * 5,
        out_shape=[sds((tokens, hg), BF), sds((tokens, hg), BF), sds((tokens, 256), F32)]
        + [sds((tokens, 256), BF)] * 5,
        scratch_shapes=[pltpu.VMEM((768, hg), BF), pltpu.VMEM((hg, 768), BF), pltpu.VMEM((hg, 768), BF)],
        compiler_params=pltpu.CompilerParams(vmem_limit_bytes=40 * 2**20),
        cost_estimate=pl.CostEstimate(
            flops=8 * tokens * hg * 768, bytes_accessed=18 * 2**20, transcendentals=tokens * hg),
        name="mid",
    )(mu, xg, *recv, *recv, z, w_up, v_up, w_down, u_down)


def wgrad_kernel(mu_ref, xg_ref, r0, r1, r2, r3, k0, k1, k2, k3, z_ref, hid_ref, gp_ref,
                 gwd_ref, gwu_ref, acc_d, acc_u):
    step = pl.program_id(0)

    @pl.when(step == 0)
    def _():
        acc_d[...] = jnp.zeros_like(acc_d)
        acc_u[...] = jnp.zeros_like(acc_u)

    refs = (xg_ref, r0, r1, r2, r3, z_ref)
    x6 = jnp.concatenate([r[:, 0:128] for r in refs], axis=1)
    gy6 = jnp.concatenate([r[:, 128:256] for r in refs], axis=1)
    acc_d[...] += matmul_tn(hid_ref[...], gy6)
    acc_u[...] += matmul_tn(x6, gp_ref[...])

    @pl.when(step == pl.num_programs(0) - 1)
    def _():
        for k in range(6):
            lo = 128 * k
            down = acc_d[:, lo:lo + 128]
            up = acc_u[lo:lo + 128, :]
            if 1 <= k <= 4:
                down = down * (k0, k1, k2, k3)[k - 1][k - 1:k, 0:128].astype(F32)
                up = up * mu_ref[k - 1]
            gwd_ref[k] = down.astype(BF)
            gwu_ref[k] = up.astype(BF)


def wgrad(mu, xg, recv, z, hidden, grad_pre):
    tokens, hg = hidden.shape
    row = lambda width: pl.BlockSpec((TILE, width), lambda i: (i, 0))
    mask_rows = pl.BlockSpec((PAD, 256), lambda i: (tokens // PAD, 0))
    sds = jax.ShapeDtypeStruct
    return pl.pallas_call(
        wgrad_kernel,
        grid=(tokens // TILE,),
        in_specs=[pl.BlockSpec(memory_space=pltpu.SMEM)] + [row(256)] * 5 + [mask_rows] * 4 + [row(256)]
        + [row(hg), row(hg)],
        out_specs=[pl.BlockSpec((6, hg, 128), lambda i: (0, 0, 0)), pl.BlockSpec((6, 128, hg), lambda i: (0, 0, 0))],
        out_shape=[sds((6, hg, 128), BF), sds((6, 128, hg), BF)],
        scratch_shapes=[pltpu.VMEM((hg, 768), F32), pltpu.VMEM((768, hg), F32)],
        compiler_params=pltpu.CompilerParams(vmem_limit_bytes=40 * 2**20),
        cost_estimate=pl.CostEstimate(flops=4 * tokens * hg * 768, bytes_accessed=14 * 2**20, transcendentals=0),
        name="wgrad",
    )(mu, xg, *recv, *recv, z, hidden, grad_pre)


def per_device(activations, w_up, w_down, u_up, v_up, u_down, v_down, mask_up, mask_down, grad_y):
    levels = mask_up.shape[0]
    tokens = activations.shape[0]
    mu = mask_up[:, 0].astype(F32)
    md = mask_down[:, 0].astype(F32)
    mask_rows = jnp.broadcast_to(jnp.pad(mask_down, ((0, PAD - levels), (0, 0))).astype(BF), (PAD, 256))
    xg = jnp.concatenate([jnp.concatenate([activations, grad_y], axis=1), mask_rows], axis=0)
    recv = [swapped(xg, *LEVEL_AXES[k]) for k in range(levels)]
    part = jnp.concatenate([matmul(activations, u_up), matmul_nt(grad_y, v_down)], axis=1).astype(BF)
    z = sum_over_mp(part)
    hidden, grad_pre, own, s0, s1, s2, s3, part2 = mid(mu, xg, recv, z, w_up, v_up, w_down, u_down)
    back = [swapped(s, *LEVEL_AXES[k]) for k, s in enumerate((s0, s1, s2, s3))]
    gwd, gwu = wgrad(mu, xg, recv, z, hidden, grad_pre)
    gwd_other = swapped(gwd, "dp", 1)
    gwu_other = swapped(gwu, "dp", 1)
    z2 = sum_over_mp(part2)
    z_down, gz_up = z2[:, 0:128], z2[:, 128:256]
    low = jnp.stack([matmul_tn(z_down, grad_y), matmul_tn(activations, gz_up)]).astype(BF)
    low_other = swapped(low, "dp", 1)
    out = own[:, 0:128] + matmul(z_down, v_down)
    grad_in = own[:, 128:256] + matmul_nt(gz_up, u_up)
    for k in range(levels):
        out = out + md[k] * back[k][:, 0:128].astype(F32)
        grad_in = grad_in + back[k][:, 128:256].astype(F32)
    g_down = gwd.astype(F32) + gwd_other.astype(F32)
    g_up = gwu.astype(F32) + gwu_other.astype(F32)
    g_low = low.astype(F32) + low_other.astype(F32)
    return (out.astype(BF), grad_in.astype(BF), g_up[0:5], g_down[0:5], g_low[1], g_up[5], g_down[5], g_low[0])


def solution(mesh):
    fine = jax.sharding.Mesh(mesh.devices.reshape(2, 4, 2, 4, 2), ("dp", "y", "xl", "z", "c"))
    mp = ("y", "xl", "z", "c")
    tok = P("dp", mp)
    rows, cols = P(mp, None), P(None, mp)
    up3, down3 = P(None, None, mp), P(None, mp, None)
    return jax.shard_map(
        per_device,
        mesh=fine,
        in_specs=(tok, up3, down3, rows, cols, rows, cols, cols, cols, tok),
        out_specs=(tok, tok, up3, down3, rows, cols, rows, cols),
        check_vma=False,
    )
```

```python
import jax
import jax.numpy as jnp
from jax import lax
from jax.experimental import pallas as pl
from jax.experimental.pallas import tpu as pltpu
from jax.sharding import PartitionSpec as P

BF = jnp.bfloat16
F32 = jnp.float32
LEVEL_AXES = (("c", 1), ("z", 1), ("z", 2), ("xl", 1))
BOARD = ("y", "z")
CHIPS = ("y", "xl", "z")
PAD = 16
TILE = 512
GELU_C = 0.7978845608028654
GELU_A = 0.044715


def cost(flops, bytes_accessed, transcendentals):
    return pl.CostEstimate(flops=int(8 * flops), bytes_accessed=int(8 * bytes_accessed), transcendentals=0)


def swapped(array, axis, bit):
    return lax.ppermute(array, axis, [(i, i ^ bit) for i in range(lax.axis_size(axis))])


def matmul(left, right):
    return jnp.dot(left, right, preferred_element_type=F32)


def matmul_nt(left, right):
    return lax.dot_general(left, right, (((1,), (1,)), ((), ())), preferred_element_type=F32)


def matmul_tn(left, right):
    return lax.dot_general(left, right, (((0,), (0,)), ((), ())), preferred_element_type=F32)


def whole(array):
    return pl.BlockSpec(array.shape, lambda *i, n=array.ndim: (0,) * n)


def shape(dims, dtype=BF):
    return jax.ShapeDtypeStruct(dims, dtype)


SMEM = pl.BlockSpec(memory_space=pltpu.SMEM)
ANY = pl.BlockSpec(memory_space=pl.ANY)
LIMIT = pltpu.CompilerParams(vmem_limit_bytes=40 * 2**20)


def first_kernel(core_ref, md_ref, x_ref, gy_ref, uu_ref, vd_ref, gym_ref, mine_ref, other_ref):
    tokens = x_ref.shape[0]
    half = tokens // 2
    for out, which in ((other_ref, 1 - core_ref[0]), (mine_ref, core_ref[0])):
        rows = pl.ds(pl.multiple_of(which * half, half), half)
        out[:, 0:128] = matmul(x_ref[rows, :], uu_ref[...]).astype(BF)
        out[:, 128:256] = matmul_nt(gy_ref[rows, :], vd_ref[...]).astype(BF)
    gym_ref[0:tokens, :] = gy_ref[...]
    row = lax.broadcasted_iota(jnp.int32, (PAD, 128), 0)
    masks = jnp.zeros((PAD, 128), F32)
    for k in range(len(LEVEL_AXES)):
        masks = jnp.where(row == k, md_ref[k], masks)
    gym_ref[tokens:tokens + PAD, :] = masks.astype(BF)


def first(core, md, x, gy, u_up, v_down):
    tokens = x.shape[0]
    return pl.pallas_call(
        first_kernel,
        in_specs=[SMEM, SMEM, whole(x), whole(gy), whole(u_up), whole(v_down)],
        out_shape=[shape((tokens + PAD, 128)), shape((tokens // 2, 256)), shape((tokens // 2, 256))],
        compiler_params=LIMIT,
        cost_estimate=cost(flops=4 * tokens * 128 * 128, bytes_accessed=3 * 2**20, transcendentals=0),
        name="first",
    )(core, md, x, gy, u_up, v_down)


def gate_kernel(*refs):
    pass


def gate(array, *arrived):
    return pl.pallas_call(
        gate_kernel,
        in_specs=[ANY] * (1 + len(arrived)),
        out_specs=ANY,
        out_shape=shape(array.shape, array.dtype),
        input_output_aliases={0: 0},
        cost_estimate=cost(flops=0, bytes_accessed=0, transcendentals=0),
        name="gate",
    )(array, *arrived)


def pair_kernel(a_ref, b_ref, out_ref):
    out_ref[...] = (a_ref[...].astype(F32) + b_ref[...].astype(F32)).astype(BF)


def pair_sum(a, b):
    return pl.pallas_call(
        pair_kernel,
        in_specs=[whole(a), whole(b)],
        out_shape=shape(a.shape),
        compiler_params=LIMIT,
        cost_estimate=cost(flops=a.size, bytes_accessed=6 * a.size, transcendentals=0),
        name="pair_sum",
    )(a, b)


def board_kernel(split_ref, *rest):
    out_ref = rest[-1]
    out_ref[...] = jnp.sum(split_ref[...].astype(F32), axis=0)


def board_sum(split, *arrived):
    return pl.pallas_call(
        board_kernel,
        in_specs=[whole(split)] + [ANY] * len(arrived),
        out_shape=shape(split.shape[1:], F32),
        compiler_params=LIMIT,
        cost_estimate=cost(flops=split.size, bytes_accessed=2 * split.size, transcendentals=0),
        name="board_sum",
    )(split, *arrived)


def spread_kernel(a_ref, b_ref, *rest):
    out_ref = rest[-1]
    total = (a_ref[...] + b_ref[...]).astype(BF)
    out_ref[...] = jnp.broadcast_to(total[None], out_ref.shape)


def spread_sum(a, b, *arrived):
    out = shape((axes_size(BOARD),) + a.shape)
    return pl.pallas_call(
        spread_kernel,
        in_specs=[whole(a), whole(b)] + [ANY] * len(arrived),
        out_shape=out,
        compiler_params=LIMIT,
        cost_estimate=cost(flops=a.size, bytes_accessed=2 * out.size, transcendentals=0),
        name="spread_sum",
    )(a, b, *arrived)


def relay_kernel(mask_ref, near_ref, far_ref, *rest):
    send_ref = rest[-1]
    near, far = near_ref[...].astype(F32), far_ref[...].astype(F32)
    near_mask = mask_ref[1:2, :].astype(F32)
    far_mask = mask_ref[2:3, :].astype(F32)
    send_ref[:, 0:128] = (near[:, 0:128] * near_mask + far[:, 0:128] * far_mask).astype(BF)
    send_ref[:, 128:256] = (near[:, 128:256] + far[:, 128:256]).astype(BF)


def relay_sum(near_recv, near, far, *arrived):
    tokens = near.shape[0]
    mask_rows = pl.BlockSpec((PAD, 128), lambda *i: (tokens // PAD, 0))
    return pl.pallas_call(
        relay_kernel,
        grid=(1,),
        in_specs=[mask_rows, whole(near), whole(far)] + [ANY] * len(arrived),
        out_specs=whole(near),
        out_shape=shape(near.shape),
        compiler_params=LIMIT,
        cost_estimate=cost(flops=4 * near.size, bytes_accessed=8 * near.size, transcendentals=0),
        name="relay_sum",
    )(near_recv, near, far, *arrived)


def axes_size(axes):
    size = 1
    for axis in axes:
        size *= lax.axis_size(axis)
    return size


def to_chips(array, axes):
    chips = axes_size(axes)
    rows, width = array.shape
    return lax.all_to_all(array.reshape(chips, rows // chips, width), axes, 0, 0, tiled=False)


def from_chips(spread, axes):
    return lax.all_to_all(spread, axes, 0, 0, tiled=False).reshape(-1, spread.shape[2])


def chip_sum_kernel(split_ref, *rest):
    out_ref = rest[-1]
    total = jnp.sum(split_ref[...].astype(F32), axis=0).astype(BF)
    out_ref[...] = jnp.broadcast_to(total[None], out_ref.shape)


def chip_sum(split, *arrived):
    return pl.pallas_call(
        chip_sum_kernel,
        in_specs=[whole(split)] + [ANY] * len(arrived),
        out_shape=shape(split.shape),
        compiler_params=LIMIT,
        cost_estimate=cost(flops=split.size, bytes_accessed=4 * split.size, transcendentals=0),
        name="chip_sum",
    )(split, *arrived)


def mid_kernel(mu_ref, core_ref, x_ref, x0, x1, x2, x3, gy_ref, g0, g1, g2, g3, k0, k1, k2, k3, za_ref, zb_ref, wu_ref, vu_ref, wd_ref, ud_ref,
               own_ref, s0, s1, s2, s3, part_ref, hid_ref, gp_ref, wu6, wd6, wdm6):
    step, steps = pl.program_id(0), pl.num_programs(0)

    @pl.when(step == 0)
    def _():
        wu6[0:128, :] = wu_ref[0]
        wd6[:, 0:128] = wd_ref[0]
        wdm6[:, 0:128] = wd_ref[0]
        for k, mask_rows in enumerate((k0, k1, k2, k3)):
            lo = 128 * (k + 1)
            wu6[lo:lo + 128, :] = (wu_ref[k + 1].astype(F32) * mu_ref[k]).astype(BF)
            wd6[:, lo:lo + 128] = wd_ref[k + 1]
            wdm6[:, lo:lo + 128] = (wd_ref[k + 1].astype(F32) * mask_rows[k:k + 1, :].astype(F32)).astype(BF)
        wu6[640:768, :] = vu_ref[...]
        wd6[:, 640:768] = ud_ref[...]
        wdm6[:, 640:768] = ud_ref[...]

    half = (2 * step) // steps
    z = jnp.where(half == core_ref[0], za_ref[...], zb_ref[...])
    x6 = jnp.concatenate([r[...] for r in (x_ref, x0, x1, x2, x3)] + [z[:, 0:128]], axis=1)
    gy6 = jnp.concatenate([r[...] for r in (gy_ref, g0, g1, g2, g3)] + [z[:, 128:256]], axis=1)
    pre = matmul(x6, wu6[...])
    square = pre * pre
    tanh = jnp.tanh(GELU_C * pre * (1.0 + GELU_A * square))
    cdf = 0.5 * (1.0 + tanh)
    hidden = (pre * cdf).astype(BF)
    hid_ref[...] = hidden
    slope = cdf + (0.5 * GELU_C) * pre * (1.0 - tanh * tanh) * (1.0 + (3.0 * GELU_A) * square)
    grad_hid = matmul_nt(gy6, wdm6[...])
    grad_pre = (grad_hid * slope).astype(BF)
    gp_ref[...] = grad_pre
    down = matmul(hidden, wd6[...])
    back = matmul_nt(grad_pre, wu6[...])
    own_ref[:, 0:128] = down[:, 0:128]
    own_ref[:, 128:256] = back[:, 0:128]
    for k, send in enumerate((s0, s1, s2, s3)):
        lo = 128 * (k + 1)
        send[:, 0:128] = down[:, lo:lo + 128].astype(BF)
        send[:, 128:256] = back[:, lo:lo + 128].astype(BF)
    part_ref[:, 0:128] = down[:, 640:768].astype(BF)
    part_ref[:, 128:256] = back[:, 640:768].astype(BF)


def weights_kernel(mu_ref, core_ref, x_ref, x0, x1, x2, x3, gy_ref, g0, g1, g2, g3, k0, k1, k2, k3, za_ref, zb_ref,
                   hid_ref, gp_ref, held_in, gwd_ref, gwu_ref, held_out, acc_d, acc_u):
    step, steps = pl.program_id(0), pl.num_programs(0)

    @pl.when(step == 0)
    def _():
        acc_d[...] = jnp.zeros_like(acc_d)
        acc_u[...] = jnp.zeros_like(acc_u)

    z = jnp.where((2 * step) // steps == core_ref[0], za_ref[...], zb_ref[...])
    x6 = jnp.concatenate([r[...] for r in (x_ref, x0, x1, x2, x3)] + [z[:, 0:128]], axis=1)
    gy6 = jnp.concatenate([r[...] for r in (gy_ref, g0, g1, g2, g3)] + [z[:, 128:256]], axis=1)
    acc_d[...] += matmul_tn(hid_ref[...], gy6)
    acc_u[...] += matmul_tn(x6, gp_ref[...])

    @pl.when(step == steps - 1)
    def _():
        for k in range(6):
            lo = 128 * k
            g_down = acc_d[:, lo:lo + 128]
            g_up = acc_u[lo:lo + 128, :]
            if 1 <= k <= 4:
                g_down = g_down * (k0, k1, k2, k3)[k - 1][k - 1:k, :].astype(F32)
                g_up = g_up * mu_ref[k - 1]
            gwd_ref[k] = g_down.astype(BF)
            gwu_ref[k] = g_up.astype(BF)


def weights(mu, core, x, gy, xs, gys, za, zb, hidden, grad_pre, held):
    tokens, hg = hidden.shape
    steps = tokens // TILE
    thin = pl.BlockSpec((TILE, 128), lambda i: (i, 0))
    wide = pl.BlockSpec((TILE, hg), lambda i: (i, 0))
    z_row = pl.BlockSpec((TILE, 256), lambda i: (lax.rem(i, steps // 2), 0))
    mask_rows = pl.BlockSpec((PAD, 128), lambda i: (tokens // PAD, 0))
    grads = [shape((6, hg, 128)), shape((6, 128, hg))]
    return pl.pallas_call(
        weights_kernel,
        grid=(steps,),
        in_specs=[SMEM, SMEM] + [thin] * 10 + [mask_rows] * 4 + [z_row] * 2 + [wide] * 2 + [ANY],
        out_specs=[whole(g) for g in grads] + [ANY],
        out_shape=grads + [shape(held.shape)],
        input_output_aliases={20: 2},
        scratch_shapes=[pltpu.VMEM((hg, 768), F32), pltpu.VMEM((768, hg), F32)],
        compiler_params=pltpu.CompilerParams(vmem_limit_bytes=56 * 2**20),
        cost_estimate=cost(flops=4 * tokens * hg * 768, bytes_accessed=14 * 2**20, transcendentals=0),
        name="weights",
    )(mu, core, x, *xs, gy, *gys, *gys, za, zb, hidden, grad_pre, held)


def mid(mu, core, x, gy, xs, gys, za, zb, w_up, v_up, w_down, u_down):
    tokens = 2 * za.shape[0]
    hg = w_up.shape[2]
    steps = tokens // TILE
    row = pl.BlockSpec((TILE, 256), lambda i: (i, 0))
    thin = pl.BlockSpec((TILE, 128), lambda i: (i, 0))
    z_row = pl.BlockSpec((TILE, 256), lambda i: (lax.rem(i, steps // 2), 0))
    mask_rows = pl.BlockSpec((PAD, 128), lambda i: (tokens // PAD, 0))
    wide = pl.BlockSpec((TILE, hg), lambda i: (i, 0))
    return pl.pallas_call(
        mid_kernel,
        grid=(steps,),
        in_specs=[SMEM, SMEM] + [thin] * 10 + [mask_rows] * 4 + [z_row] * 2
        + [whole(w_up), whole(v_up), whole(w_down), whole(u_down)],
        out_specs=[row] * 6 + [wide] * 2,
        out_shape=[shape((tokens, 256), F32)] + [shape((tokens, 256))] * 5
        + [shape((tokens, hg))] * 2,
        scratch_shapes=[pltpu.VMEM((768, hg), BF), pltpu.VMEM((hg, 768), BF), pltpu.VMEM((hg, 768), BF)],
        compiler_params=pltpu.CompilerParams(vmem_limit_bytes=56 * 2**20),
        cost_estimate=cost(
            flops=8 * tokens * hg * 768, bytes_accessed=20 * 2**20, transcendentals=tokens * hg),
        name="mid",
    )(mu, core, x, *xs, gy, *gys, *gys, za, zb, w_up, v_up, w_down, u_down)


def grad_kernel(a_ref, b_ref, five_ref, one_ref):
    total = a_ref[...].astype(F32) + b_ref[...].astype(F32)
    five_ref[...] = total[0:5]
    one_ref[...] = total[5]


def grad_sum(a, b):
    dims = a.shape[1:]
    return pl.pallas_call(
        grad_kernel,
        in_specs=[whole(a), whole(b)],
        out_shape=[shape((5,) + dims, F32), shape(dims, F32)],
        compiler_params=LIMIT,
        cost_estimate=cost(flops=a.size, bytes_accessed=8 * a.size, transcendentals=0),
        name="grad_sum",
    )(a, b)


def low_kernel(core_ref, x_ref, gy_ref, za_ref, zb_ref, *rest):
    out_ref = rest[-1]
    first_half = core_ref[0] == 0
    half = za_ref.shape[0]
    za, zb = za_ref[...], zb_ref[...]
    z0, z1 = jnp.where(first_half, za, zb), jnp.where(first_half, zb, za)
    out_ref[0] = (matmul_tn(z0[:, 0:128], gy_ref[0:half]) + matmul_tn(z1[:, 0:128], gy_ref[half:])).astype(BF)
    out_ref[1] = (matmul_tn(x_ref[0:half], z0[:, 128:256]) + matmul_tn(x_ref[half:], z1[:, 128:256])).astype(BF)


def low_grads(core, x, gy, za, zb, *arrived):
    return pl.pallas_call(
        low_kernel,
        in_specs=[SMEM, whole(x), whole(gy), whole(za), whole(zb)] + [ANY] * len(arrived),
        out_shape=shape((2, 128, 128)),
        compiler_params=LIMIT,
        cost_estimate=cost(flops=4 * x.size * 128, bytes_accessed=4 * x.size, transcendentals=0),
        name="low_grads",
    )(core, x, gy, za, zb, *arrived)


def last_kernel(md_ref, core_ref, own_ref, b0, b1, b3, za_ref, zb_ref, vd_ref, uu_ref, out_ref, gx_ref):
    step, steps = pl.program_id(0), pl.num_programs(0)
    z = jnp.where((2 * step) // steps == core_ref[0], za_ref[...], zb_ref[...])
    out = own_ref[:, 0:128] + matmul(z[:, 0:128], vd_ref[...])
    out = out + md_ref[0] * b0[:, 0:128].astype(F32) + md_ref[3] * b3[:, 0:128].astype(F32)
    out_ref[...] = (out + b1[:, 0:128].astype(F32)).astype(BF)
    gx = own_ref[:, 128:256] + matmul_nt(z[:, 128:256], uu_ref[...])
    gx = gx + b0[:, 128:256].astype(F32) + b3[:, 128:256].astype(F32)
    gx_ref[...] = (gx + b1[:, 128:256].astype(F32)).astype(BF)


def last(md, core, own, b0, b1, b3, za, zb, v_down, u_up):
    tokens = own.shape[0]
    steps = tokens // TILE
    row = pl.BlockSpec((TILE, 256), lambda i: (i, 0))
    z_row = pl.BlockSpec((TILE, 256), lambda i: (lax.rem(i, steps // 2), 0))
    out = pl.BlockSpec((TILE, 128), lambda i: (i, 0))
    return pl.pallas_call(
        last_kernel,
        grid=(steps,),
        in_specs=[SMEM, SMEM] + [row] * 4 + [z_row] * 2 + [whole(v_down), whole(u_up)],
        out_specs=[out, out],
        out_shape=[shape((tokens, 128))] * 2,
        compiler_params=LIMIT,
        cost_estimate=cost(flops=4 * tokens * 128 * 128, bytes_accessed=7 * 2**20, transcendentals=0),
        name="last",
    )(md, core, own, b0, b1, b3, za, zb, v_down, u_up)


def per_device(activations, w_up, w_down, u_up, v_up, u_down, v_down, mask_up, mask_down, grad_y):
    mu = mask_up[:, 0].astype(F32)
    md = mask_down[:, 0].astype(F32)
    core = lax.axis_index("c").reshape(1)
    x0 = swapped(activations, "c", 1)
    x1 = swapped(activations, "z", 1)
    x3 = swapped(activations, "xl", 1)
    x2 = swapped(x1, "z", 3)
    gym, mine, other = first(core, md, activations, grad_y, u_up, v_down)
    split = to_chips(pair_sum(mine, swapped(other, "c", 1)), CHIPS)
    gym = gate(gym, x1, x3)
    g0 = swapped(gym, "c", 1)
    g1 = swapped(gym, "z", 1)
    g3 = swapped(gym, "xl", 1)
    g2 = swapped(g1, "z", 3)
    za = from_chips(chip_sum(split, x2, g3), CHIPS)
    zb = swapped(za, "c", 1)
    own, s0, s1, s2, s3, part, hidden, grad_pre = mid(
        mu, core, activations, grad_y, (x0, x1, x2, x3), (g0, g1, g2, g3), za, zb, w_up, v_up, w_down, u_down)
    half = part.shape[0] // 2
    mine = lax.dynamic_slice_in_dim(part, core[0] * half, half, 0)
    other = lax.dynamic_slice_in_dim(part, (1 - core[0]) * half, half, 0)
    b3 = swapped(s3, "xl", 1)
    b0 = swapped(s0, "c", 1)
    gwd, gwu, s2 = weights(
        mu, core, activations, grad_y, (x0, x1, x2, x3), (g0, g1, g2, g3), za, zb, hidden, grad_pre, s2)
    far = swapped(s2, "z", 3)
    gwd_other = swapped(gwd, "dp", 1)
    gwu_other = swapped(gwu, "dp", 1)
    total = board_sum(to_chips(pair_sum(mine, swapped(other, "c", 1)), BOARD), b3)
    spread = spread_sum(total, swapped(total, "xl", 1), far, gwd_other)
    za = from_chips(spread, BOARD)
    near = relay_sum(g1, s1, far)
    b1 = swapped(near, "z", 1)
    zb = swapped(za, "c", 1)
    low = low_grads(core, activations, grad_y, za, zb, gwu_other, b1)
    low_other = swapped(low, "dp", 1)
    out, grad_x = last(md, core, own, b0, b1, b3, za, zb, v_down, u_up)
    g_down, g_u_down = grad_sum(gwd, gwd_other)
    g_up, g_v_up = grad_sum(gwu, gwu_other)
    g_low = low.astype(F32) + low_other.astype(F32)
    return (out, grad_x, g_up, g_down, g_low[1], g_v_up, g_u_down, g_low[0])


def solution(mesh):
    fine = jax.sharding.Mesh(mesh.devices.reshape(2, 4, 2, 4, 2), ("dp", "y", "xl", "z", "c"))
    mp = ("y", "xl", "z", "c")
    tok = P("dp", mp)
    rows, cols = P(mp, None), P(None, mp)
    up3, down3 = P(None, None, mp), P(None, mp, None)
    return jax.shard_map(
        per_device,
        mesh=fine,
        in_specs=(tok, up3, down3, rows, cols, rows, cols, cols, cols, tok),
        out_specs=(tok, tok, up3, down3, rows, cols, rows, cols),
        check_vma=False,
    )
```

```python
import jax
import jax.numpy as jnp
from jax import lax
from jax.experimental import pallas as pl
from jax.experimental.pallas import tpu as pltpu
from jax.sharding import PartitionSpec as P

BF = jnp.bfloat16
F32 = jnp.float32
LEVEL_AXES = (("c", 1), ("z", 1), ("z", 2), ("xl", 1))
BOARD = ("y", "z")
CHIPS = ("y", "xl", "z")
PAD = 16
TILE = 512
GELU_C = 0.7978845608028654
GELU_A = 0.044715


def swapped(array, axis, bit):
    return lax.ppermute(array, axis, [(i, i ^ bit) for i in range(lax.axis_size(axis))])


def matmul(left, right):
    return jnp.dot(left, right, preferred_element_type=F32)


def matmul_nt(left, right):
    return lax.dot_general(left, right, (((1,), (1,)), ((), ())), preferred_element_type=F32)


def matmul_tn(left, right):
    return lax.dot_general(left, right, (((0,), (0,)), ((), ())), preferred_element_type=F32)


def whole(array):
    return pl.BlockSpec(array.shape, lambda *i, n=array.ndim: (0,) * n)


def shape(dims, dtype=BF):
    return jax.ShapeDtypeStruct(dims, dtype)


SMEM = pl.BlockSpec(memory_space=pltpu.SMEM)
ANY = pl.BlockSpec(memory_space=pl.ANY)
LIMIT = pltpu.CompilerParams(vmem_limit_bytes=40 * 2**20)


def first_kernel(core_ref, md_ref, x_ref, gy_ref, uu_ref, vd_ref, gym_ref, mine_ref, other_ref):
    tokens = x_ref.shape[0]
    half = tokens // 2
    for out, which in ((other_ref, 1 - core_ref[0]), (mine_ref, core_ref[0])):
        rows = pl.ds(pl.multiple_of(which * half, half), half)
        out[:, 0:128] = matmul(x_ref[rows, :], uu_ref[...]).astype(BF)
        out[:, 128:256] = matmul_nt(gy_ref[rows, :], vd_ref[...]).astype(BF)
    gym_ref[0:tokens, :] = gy_ref[...]
    row = lax.broadcasted_iota(jnp.int32, (PAD, 128), 0)
    masks = jnp.zeros((PAD, 128), F32)
    for k in range(len(LEVEL_AXES)):
        masks = jnp.where(row == k, md_ref[k], masks)
    gym_ref[tokens:tokens + PAD, :] = masks.astype(BF)


def first(core, md, x, gy, u_up, v_down):
    tokens = x.shape[0]
    return pl.pallas_call(
        first_kernel,
        in_specs=[SMEM, SMEM, whole(x), whole(gy), whole(u_up), whole(v_down)],
        out_shape=[shape((tokens + PAD, 128)), shape((tokens // 2, 256)), shape((tokens // 2, 256))],
        compiler_params=LIMIT,
        cost_estimate=pl.CostEstimate(flops=4 * tokens * 128 * 128, bytes_accessed=3 * 2**20, transcendentals=0),
        name="first",
    )(core, md, x, gy, u_up, v_down)


def gate_kernel(*refs):
    pass


def gate(array, *arrived):
    return pl.pallas_call(
        gate_kernel,
        in_specs=[ANY] * (1 + len(arrived)),
        out_specs=ANY,
        out_shape=shape(array.shape, array.dtype),
        input_output_aliases={0: 0},
        cost_estimate=pl.CostEstimate(flops=0, bytes_accessed=0, transcendentals=0),
        name="gate",
    )(array, *arrived)


def pair_kernel(a_ref, b_ref, out_ref):
    out_ref[...] = (a_ref[...].astype(F32) + b_ref[...].astype(F32)).astype(BF)


def pair_sum(a, b):
    return pl.pallas_call(
        pair_kernel,
        in_specs=[whole(a), whole(b)],
        out_shape=shape(a.shape),
        compiler_params=LIMIT,
        cost_estimate=pl.CostEstimate(flops=a.size, bytes_accessed=6 * a.size, transcendentals=0),
        name="pair_sum",
    )(a, b)


def board_kernel(split_ref, *rest):
    out_ref = rest[-2]
    out_ref[...] = jnp.sum(split_ref[...].astype(F32), axis=0)


def board_sum(split, held, *arrived):
    return pl.pallas_call(
        board_kernel,
        in_specs=[whole(split), ANY] + [ANY] * len(arrived),
        out_specs=[pl.BlockSpec(split.shape[1:], lambda: (0, 0)), ANY],
        out_shape=[shape(split.shape[1:], F32), shape(held.shape)],
        input_output_aliases={1: 1},
        compiler_params=LIMIT,
        cost_estimate=pl.CostEstimate(flops=split.size, bytes_accessed=2 * split.size, transcendentals=0),
        name="board_sum",
    )(split, held, *arrived)


def spread_kernel(a_ref, b_ref, *rest):
    out_ref = rest[-1]
    total = (a_ref[...] + b_ref[...]).astype(BF)
    out_ref[...] = jnp.broadcast_to(total[None], out_ref.shape)


def spread_sum(a, b, *arrived):
    out = shape((axes_size(BOARD),) + a.shape)
    return pl.pallas_call(
        spread_kernel,
        in_specs=[whole(a), whole(b)] + [ANY] * len(arrived),
        out_shape=out,
        compiler_params=LIMIT,
        cost_estimate=pl.CostEstimate(flops=a.size, bytes_accessed=2 * out.size, transcendentals=0),
        name="spread_sum",
    )(a, b, *arrived)


def relay_kernel(mask_ref, near_ref, far_ref, *rest):
    send_ref = rest[-1]
    near, far = near_ref[...].astype(F32), far_ref[...].astype(F32)
    near_mask = mask_ref[1:2, :].astype(F32)
    far_mask = mask_ref[2:3, :].astype(F32)
    send_ref[:, 0:128] = (near[:, 0:128] * near_mask + far[:, 0:128] * far_mask).astype(BF)
    send_ref[:, 128:256] = (near[:, 128:256] + far[:, 128:256]).astype(BF)


def relay_sum(near_recv, near, far, *arrived):
    tokens = near.shape[0]
    mask_rows = pl.BlockSpec((PAD, 128), lambda *i: (tokens // PAD, 0))
    return pl.pallas_call(
        relay_kernel,
        grid=(1,),
        in_specs=[mask_rows, whole(near), whole(far)] + [ANY] * len(arrived),
        out_specs=whole(near),
        out_shape=shape(near.shape),
        compiler_params=LIMIT,
        cost_estimate=pl.CostEstimate(flops=4 * near.size, bytes_accessed=8 * near.size, transcendentals=0),
        name="relay_sum",
    )(near_recv, near, far, *arrived)


def axes_size(axes):
    size = 1
    for axis in axes:
        size *= lax.axis_size(axis)
    return size


def to_chips(array, axes):
    chips = axes_size(axes)
    rows, width = array.shape
    return lax.all_to_all(array.reshape(chips, rows // chips, width), axes, 0, 0, tiled=False)


def from_chips(spread, axes):
    return lax.all_to_all(spread, axes, 0, 0, tiled=False).reshape(-1, spread.shape[2])


def chip_sum_kernel(split_ref, *rest):
    out_ref = rest[-1]
    total = jnp.sum(split_ref[...].astype(F32), axis=0).astype(BF)
    out_ref[...] = jnp.broadcast_to(total[None], out_ref.shape)


def chip_sum(split, *arrived):
    return pl.pallas_call(
        chip_sum_kernel,
        in_specs=[whole(split)] + [ANY] * len(arrived),
        out_shape=shape(split.shape),
        compiler_params=LIMIT,
        cost_estimate=pl.CostEstimate(flops=split.size, bytes_accessed=4 * split.size, transcendentals=0),
        name="chip_sum",
    )(split, *arrived)


def mid_kernel(core_ref, mu_ref, x_ref, x0, x1, x2, x3, gy_ref, g0, g1, g2, g3, k0, k1, k2, k3, za_ref, zb_ref, wu_ref, vu_ref, wd_ref, ud_ref,
               own_ref, s0, s1, s2, s3, mine_ref, other_ref, hid_ref, gp_ref, wu6, wd6, wdm6):
    step, steps = pl.program_id(0), pl.num_programs(0)

    @pl.when(step == 0)
    def _():
        wu6[0:128, :] = wu_ref[0]
        wd6[:, 0:128] = wd_ref[0]
        wdm6[:, 0:128] = wd_ref[0]
        for k, mask_rows in enumerate((k0, k1, k2, k3)):
            lo = 128 * (k + 1)
            wu6[lo:lo + 128, :] = (wu_ref[k + 1].astype(F32) * mu_ref[k]).astype(BF)
            wd6[:, lo:lo + 128] = wd_ref[k + 1]
            wdm6[:, lo:lo + 128] = (wd_ref[k + 1].astype(F32) * mask_rows[k:k + 1, :].astype(F32)).astype(BF)
        wu6[640:768, :] = vu_ref[...]
        wd6[:, 640:768] = ud_ref[...]
        wdm6[:, 640:768] = ud_ref[...]

    half = (2 * step) // steps
    z = jnp.where(half == core_ref[0], za_ref[...], zb_ref[...])
    x6 = jnp.concatenate([r[...] for r in (x_ref, x0, x1, x2, x3)] + [z[:, 0:128]], axis=1)
    gy6 = jnp.concatenate([r[...] for r in (gy_ref, g0, g1, g2, g3)] + [z[:, 128:256]], axis=1)
    pre = matmul(x6, wu6[...])
    square = pre * pre
    tanh = jnp.tanh(GELU_C * pre * (1.0 + GELU_A * square))
    cdf = 0.5 * (1.0 + tanh)
    hidden = (pre * cdf).astype(BF)
    hid_ref[...] = hidden
    slope = cdf + (0.5 * GELU_C) * pre * (1.0 - tanh * tanh) * (1.0 + (3.0 * GELU_A) * square)
    grad_hid = matmul_nt(gy6, wdm6[...])
    grad_pre = (grad_hid * slope).astype(BF)
    gp_ref[...] = grad_pre
    down = matmul(hidden, wd6[...])
    back = matmul_nt(grad_pre, wu6[...])
    own_ref[:, 0:128] = down[:, 0:128]
    own_ref[:, 128:256] = back[:, 0:128]
    for k, send in enumerate((s0, s1, s2, s3)):
        lo = 128 * (k + 1)
        send[:, 0:128] = down[:, lo:lo + 128].astype(BF)
        send[:, 128:256] = back[:, lo:lo + 128].astype(BF)
    part = jnp.concatenate([down[:, 640:768], back[:, 640:768]], axis=1).astype(BF)

    @pl.when(half == core_ref[0])
    def _():
        mine_ref[...] = part

    @pl.when(half != core_ref[0])
    def _():
        other_ref[...] = part


def weights_kernel(mu_ref, core_ref, x_ref, x0, x1, x2, x3, gy_ref, g0, g1, g2, g3, k0, k1, k2, k3, za_ref, zb_ref,
                   hid_ref, gp_ref, *rest):
    gwd_ref, gwu_ref, acc_d, acc_u = rest[-4:]
    step, steps = pl.program_id(0), pl.num_programs(0)

    @pl.when(step == 0)
    def _():
        acc_d[...] = jnp.zeros_like(acc_d)
        acc_u[...] = jnp.zeros_like(acc_u)

    z = jnp.where((2 * step) // steps == core_ref[0], za_ref[...], zb_ref[...])
    x6 = jnp.concatenate([r[...] for r in (x_ref, x0, x1, x2, x3)] + [z[:, 0:128]], axis=1)
    gy6 = jnp.concatenate([r[...] for r in (gy_ref, g0, g1, g2, g3)] + [z[:, 128:256]], axis=1)
    acc_d[...] += matmul_tn(hid_ref[...], gy6)
    acc_u[...] += matmul_tn(x6, gp_ref[...])

    @pl.when(step == steps - 1)
    def _():
        for k in range(6):
            lo = 128 * k
            g_down = acc_d[:, lo:lo + 128]
            g_up = acc_u[lo:lo + 128, :]
            if 1 <= k <= 4:
                g_down = g_down * (k0, k1, k2, k3)[k - 1][k - 1:k, :].astype(F32)
                g_up = g_up * mu_ref[k - 1]
            gwd_ref[k] = g_down.astype(BF)
            gwu_ref[k] = g_up.astype(BF)


def weights(mu, core, x, gy, xs, gys, za, zb, hidden, grad_pre, *arrived):
    tokens, hg = hidden.shape
    steps = tokens // TILE
    thin = pl.BlockSpec((TILE, 128), lambda i: (i, 0))
    wide = pl.BlockSpec((TILE, hg), lambda i: (i, 0))
    z_row = pl.BlockSpec((TILE, 256), lambda i: (lax.rem(i, steps // 2), 0))
    mask_rows = pl.BlockSpec((PAD, 128), lambda i: (tokens // PAD, 0))
    grads = [shape((6, hg, 128)), shape((6, 128, hg))]
    return pl.pallas_call(
        weights_kernel,
        grid=(steps,),
        in_specs=[SMEM, SMEM] + [thin] * 10 + [mask_rows] * 4 + [z_row] * 2 + [wide] * 2 + [ANY] * len(arrived),
        out_specs=[whole(g) for g in grads],
        out_shape=grads,
        scratch_shapes=[pltpu.VMEM((hg, 768), F32), pltpu.VMEM((768, hg), F32)],
        compiler_params=pltpu.CompilerParams(vmem_limit_bytes=56 * 2**20),
        cost_estimate=pl.CostEstimate(flops=4 * tokens * hg * 768, bytes_accessed=14 * 2**20, transcendentals=0),
        name="weights",
    )(mu, core, x, *xs, gy, *gys, *gys, za, zb, hidden, grad_pre, *arrived)


def mid(mu, core, x, gy, xs, gys, za, zb, w_up, v_up, w_down, u_down):
    tokens = 2 * za.shape[0]
    hg = w_up.shape[2]
    steps = tokens // TILE
    half = steps // 2
    row = pl.BlockSpec((TILE, 256), lambda i, c: (i, 0))
    thin = pl.BlockSpec((TILE, 128), lambda i, c: (i, 0))
    wide = pl.BlockSpec((TILE, hg), lambda i, c: (i, 0))
    z_row = pl.BlockSpec((TILE, 256), lambda i, c: (lax.rem(i, half), 0))
    first_rows = lambda i: jnp.minimum(i, half - 1)
    second_rows = lambda i: jnp.maximum(i - half, 0)
    mine = pl.BlockSpec((TILE, 256), lambda i, c: (jnp.where(c[0] == 0, first_rows(i), second_rows(i)), 0))
    other = pl.BlockSpec((TILE, 256), lambda i, c: (jnp.where(c[0] == 0, second_rows(i), first_rows(i)), 0))
    mask_rows = pl.BlockSpec((PAD, 128), lambda i, c: (tokens // PAD, 0))
    return pl.pallas_call(
        mid_kernel,
        grid_spec=pltpu.PrefetchScalarGridSpec(
            num_scalar_prefetch=1,
            grid=(steps,),
            in_specs=[SMEM] + [thin] * 10 + [mask_rows] * 4 + [z_row] * 2
            + [whole(w_up), whole(v_up), whole(w_down), whole(u_down)],
            out_specs=[row] * 5 + [mine, other] + [wide] * 2,
            scratch_shapes=[pltpu.VMEM((768, hg), BF), pltpu.VMEM((hg, 768), BF), pltpu.VMEM((hg, 768), BF)],
        ),
        out_shape=[shape((tokens, 256), F32)] + [shape((tokens, 256))] * 4 + [shape((tokens // 2, 256))] * 2
        + [shape((tokens, hg))] * 2,
        compiler_params=pltpu.CompilerParams(vmem_limit_bytes=56 * 2**20),
        cost_estimate=pl.CostEstimate(
            flops=8 * tokens * hg * 768, bytes_accessed=20 * 2**20, transcendentals=tokens * hg),
        name="mid",
    )(core, mu, x, *xs, gy, *gys, *gys, za, zb, w_up, v_up, w_down, u_down)


def grad_kernel(a_ref, b_ref, five_ref, one_ref):
    total = a_ref[...].astype(F32) + b_ref[...].astype(F32)
    five_ref[...] = total[0:5]
    one_ref[...] = total[5]


def grad_sum(a, b):
    dims = a.shape[1:]
    return pl.pallas_call(
        grad_kernel,
        in_specs=[whole(a), whole(b)],
        out_shape=[shape((5,) + dims, F32), shape(dims, F32)],
        compiler_params=LIMIT,
        cost_estimate=pl.CostEstimate(flops=a.size, bytes_accessed=8 * a.size, transcendentals=0),
        name="grad_sum",
    )(a, b)


def low_kernel(core_ref, x_ref, gy_ref, za_ref, zb_ref, *rest):
    out_ref = rest[-1]
    first_half = core_ref[0] == 0
    half = za_ref.shape[0]
    za, zb = za_ref[...], zb_ref[...]
    z0, z1 = jnp.where(first_half, za, zb), jnp.where(first_half, zb, za)
    out_ref[0] = (matmul_tn(z0[:, 0:128], gy_ref[0:half]) + matmul_tn(z1[:, 0:128], gy_ref[half:])).astype(BF)
    out_ref[1] = (matmul_tn(x_ref[0:half], z0[:, 128:256]) + matmul_tn(x_ref[half:], z1[:, 128:256])).astype(BF)


def low_grads(core, x, gy, za, zb, *arrived):
    return pl.pallas_call(
        low_kernel,
        in_specs=[SMEM, whole(x), whole(gy), whole(za), whole(zb)] + [ANY] * len(arrived),
        out_shape=shape((2, 128, 128)),
        compiler_params=LIMIT,
        cost_estimate=pl.CostEstimate(flops=4 * x.size * 128, bytes_accessed=4 * x.size, transcendentals=0),
        name="low_grads",
    )(core, x, gy, za, zb, *arrived)


def last_kernel(md_ref, core_ref, own_ref, b0, b1, b3, za_ref, zb_ref, vd_ref, uu_ref, out_ref, gx_ref):
    step, steps = pl.program_id(0), pl.num_programs(0)
    z = jnp.where((2 * step) // steps == core_ref[0], za_ref[...], zb_ref[...])
    out = own_ref[:, 0:128] + matmul(z[:, 0:128], vd_ref[...])
    out = out + md_ref[0] * b0[:, 0:128].astype(F32) + md_ref[3] * b3[:, 0:128].astype(F32)
    out_ref[...] = (out + b1[:, 0:128].astype(F32)).astype(BF)
    gx = own_ref[:, 128:256] + matmul_nt(z[:, 128:256], uu_ref[...])
    gx = gx + b0[:, 128:256].astype(F32) + b3[:, 128:256].astype(F32)
    gx_ref[...] = (gx + b1[:, 128:256].astype(F32)).astype(BF)


def last(md, core, own, b0, b1, b3, za, zb, v_down, u_up):
    tokens = own.shape[0]
    steps = tokens // TILE
    row = pl.BlockSpec((TILE, 256), lambda i: (i, 0))
    z_row = pl.BlockSpec((TILE, 256), lambda i: (lax.rem(i, steps // 2), 0))
    out = pl.BlockSpec((TILE, 128), lambda i: (i, 0))
    return pl.pallas_call(
        last_kernel,
        grid=(steps,),
        in_specs=[SMEM, SMEM] + [row] * 4 + [z_row] * 2 + [whole(v_down), whole(u_up)],
        out_specs=[out, out],
        out_shape=[shape((tokens, 128))] * 2,
        compiler_params=LIMIT,
        cost_estimate=pl.CostEstimate(flops=4 * tokens * 128 * 128, bytes_accessed=7 * 2**20, transcendentals=0),
        name="last",
    )(md, core, own, b0, b1, b3, za, zb, v_down, u_up)


def per_device(activations, w_up, w_down, u_up, v_up, u_down, v_down, mask_up, mask_down, grad_y):
    mu = mask_up[:, 0].astype(F32)
    md = mask_down[:, 0].astype(F32)
    core = lax.axis_index("c").reshape(1)
    x0 = swapped(activations, "c", 1)
    x1 = swapped(activations, "z", 1)
    x3 = swapped(activations, "xl", 1)
    x2 = swapped(x1, "z", 3)
    gym, mine, other = first(core, md, activations, grad_y, u_up, v_down)
    split = to_chips(pair_sum(mine, swapped(other, "c", 1)), CHIPS)
    gym = gate(gym, x1, x3)
    g0 = swapped(gym, "c", 1)
    g1 = swapped(gym, "z", 1)
    g3 = swapped(gym, "xl", 1)
    g2 = swapped(g1, "z", 3)
    za = from_chips(chip_sum(split, x2, g3), CHIPS)
    zb = swapped(za, "c", 1)
    own, s0, s1, s2, s3, mine, other, hidden, grad_pre = mid(
        mu, core, activations, grad_y, (x0, x1, x2, x3), (g0, g1, g2, g3), za, zb, w_up, v_up, w_down, u_down)
    b3 = swapped(s3, "xl", 1)
    b0 = swapped(s0, "c", 1)
    gwd, gwu = weights(
        mu, core, activations, grad_y, (x0, x1, x2, x3), (g0, g1, g2, g3), za, zb, hidden, grad_pre)
    total, s2 = board_sum(to_chips(pair_sum(mine, swapped(other, "c", 1)), BOARD), s2, gwd)
    total_other = swapped(total, "xl", 1)
    far = swapped(s2, "z", 3)
    gwd_other = swapped(gwd, "dp", 1)
    gwu_other = swapped(gwu, "dp", 1)
    spread = spread_sum(total, total_other, b3)
    za = from_chips(spread, BOARD)
    near = relay_sum(g1, s1, far)
    b1 = swapped(near, "z", 1)
    zb = swapped(za, "c", 1)
    low = low_grads(core, activations, grad_y, za, zb)
    low_other = swapped(low, "dp", 1)
    out, grad_x = last(md, core, own, b0, b1, b3, za, zb, v_down, u_up)
    g_down, g_u_down = grad_sum(gwd, gwd_other)
    g_up, g_v_up = grad_sum(gwu, gwu_other)
    g_low = low.astype(F32) + low_other.astype(F32)
    return (out, grad_x, g_up, g_down, g_low[1], g_v_up, g_u_down, g_low[0])


def solution(mesh):
    fine = jax.sharding.Mesh(mesh.devices.reshape(2, 4, 2, 4, 2), ("dp", "y", "xl", "z", "c"))
    mp = ("y", "xl", "z", "c")
    tok = P("dp", mp)
    rows, cols = P(mp, None), P(None, mp)
    up3, down3 = P(None, None, mp), P(None, mp, None)
    return jax.shard_map(
        per_device,
        mesh=fine,
        in_specs=(tok, up3, down3, rows, cols, rows, cols, cols, cols, tok),
        out_specs=(tok, tok, up3, down3, rows, cols, rows, cols),
        check_vma=False,
    )
```

```python
import jax
import jax.numpy as jnp
from jax import lax
from jax.experimental import pallas as pl
from jax.experimental.pallas import tpu as pltpu
from jax.sharding import PartitionSpec as P

BF = jnp.bfloat16
F32 = jnp.float32
LEVEL_AXES = (("c", 1), ("z", 1), ("z", 2), ("xl", 1))
BOARD = ("y", "z")
CHIPS = ("y", "xl", "z")
PAD = 16
TILE = 512
LAST_TILE = 1024
GELU_C = 0.7978845608028654
GELU_A = 0.044715


def swapped(array, axis, bit):
    return lax.ppermute(array, axis, [(i, i ^ bit) for i in range(lax.axis_size(axis))])


def matmul(left, right):
    return jnp.dot(left, right, preferred_element_type=F32)


def matmul_nt(left, right):
    return lax.dot_general(left, right, (((1,), (1,)), ((), ())), preferred_element_type=F32)


def matmul_tn(left, right):
    return lax.dot_general(left, right, (((0,), (0,)), ((), ())), preferred_element_type=F32)


def whole(array):
    return pl.BlockSpec(array.shape, lambda *i, n=array.ndim: (0,) * n)


def shape(dims, dtype=BF):
    return jax.ShapeDtypeStruct(dims, dtype)


SMEM = pl.BlockSpec(memory_space=pltpu.SMEM)
ANY = pl.BlockSpec(memory_space=pl.ANY)
LIMIT = pltpu.CompilerParams(vmem_limit_bytes=40 * 2**20)


def first_kernel(core_ref, md_ref, x_ref, gy_ref, uu_ref, vd_ref, gym_ref, mine_ref, other_ref):
    tokens = x_ref.shape[0]
    half = tokens // 2
    for out, which in ((other_ref, 1 - core_ref[0]), (mine_ref, core_ref[0])):
        rows = pl.ds(pl.multiple_of(which * half, half), half)
        out[:, 0:128] = matmul(x_ref[rows, :], uu_ref[...]).astype(BF)
        out[:, 128:256] = matmul_nt(gy_ref[rows, :], vd_ref[...]).astype(BF)
    gym_ref[0:tokens, :] = gy_ref[...]
    row = lax.broadcasted_iota(jnp.int32, (PAD, 128), 0)
    masks = jnp.zeros((PAD, 128), F32)
    for k in range(len(LEVEL_AXES)):
        masks = jnp.where(row == k, md_ref[k], masks)
    gym_ref[tokens:tokens + PAD, :] = masks.astype(BF)


def first(core, md, x, gy, u_up, v_down):
    tokens = x.shape[0]
    return pl.pallas_call(
        first_kernel,
        in_specs=[SMEM, SMEM, whole(x), whole(gy), whole(u_up), whole(v_down)],
        out_shape=[shape((tokens + PAD, 128)), shape((tokens // 2, 256)), shape((tokens // 2, 256))],
        compiler_params=LIMIT,
        cost_estimate=pl.CostEstimate(flops=4 * tokens * 128 * 128, bytes_accessed=3 * 2**20, transcendentals=0),
        name="first",
    )(core, md, x, gy, u_up, v_down)


def gate_kernel(*refs):
    pass


def gate(array, *arrived):
    return pl.pallas_call(
        gate_kernel,
        in_specs=[ANY] * (1 + len(arrived)),
        out_specs=ANY,
        out_shape=shape(array.shape, array.dtype),
        input_output_aliases={0: 0},
        cost_estimate=pl.CostEstimate(flops=0, bytes_accessed=0, transcendentals=0),
        name="gate",
    )(array, *arrived)


def pair_kernel(a_ref, b_ref, out_ref):
    out_ref[...] = (a_ref[...].astype(F32) + b_ref[...].astype(F32)).astype(BF)


def pair_sum(a, b):
    return pl.pallas_call(
        pair_kernel,
        in_specs=[whole(a), whole(b)],
        out_shape=shape(a.shape),
        compiler_params=LIMIT,
        cost_estimate=pl.CostEstimate(flops=a.size, bytes_accessed=6 * a.size, transcendentals=0),
        name="pair_sum",
    )(a, b)


def board_kernel(split_ref, *rest):
    out_ref = rest[-2]
    out_ref[...] = jnp.sum(split_ref[...].astype(F32), axis=0)


def board_sum(split, held, *arrived):
    return pl.pallas_call(
        board_kernel,
        in_specs=[whole(split), ANY] + [ANY] * len(arrived),
        out_specs=[pl.BlockSpec(split.shape[1:], lambda: (0, 0)), ANY],
        out_shape=[shape(split.shape[1:], F32), shape(held.shape)],
        input_output_aliases={1: 1},
        compiler_params=LIMIT,
        cost_estimate=pl.CostEstimate(flops=split.size, bytes_accessed=2 * split.size, transcendentals=0),
        name="board_sum",
    )(split, held, *arrived)


def spread_kernel(a_ref, b_ref, *rest):
    out_ref = rest[-1]
    total = (a_ref[...] + b_ref[...]).astype(BF)
    out_ref[...] = jnp.broadcast_to(total[None], out_ref.shape)


def spread_sum(a, b, *arrived):
    out = shape((axes_size(BOARD),) + a.shape)
    return pl.pallas_call(
        spread_kernel,
        in_specs=[whole(a), whole(b)] + [ANY] * len(arrived),
        out_shape=out,
        compiler_params=LIMIT,
        cost_estimate=pl.CostEstimate(flops=a.size, bytes_accessed=2 * out.size, transcendentals=0),
        name="spread_sum",
    )(a, b, *arrived)


def relay_kernel(mask_ref, near_ref, far_ref, *rest):
    send_ref = rest[-1]
    near, far = near_ref[...].astype(F32), far_ref[...].astype(F32)
    near_mask = mask_ref[1:2, :].astype(F32)
    far_mask = mask_ref[2:3, :].astype(F32)
    send_ref[:, 0:128] = (near[:, 0:128] * near_mask + far[:, 0:128] * far_mask).astype(BF)
    send_ref[:, 128:256] = (near[:, 128:256] + far[:, 128:256]).astype(BF)


def relay_sum(near_recv, near, far, *arrived):
    tokens = near.shape[0]
    mask_rows = pl.BlockSpec((PAD, 128), lambda *i: (tokens // PAD, 0))
    return pl.pallas_call(
        relay_kernel,
        grid=(1,),
        in_specs=[mask_rows, whole(near), whole(far)] + [ANY] * len(arrived),
        out_specs=whole(near),
        out_shape=shape(near.shape),
        compiler_params=LIMIT,
        cost_estimate=pl.CostEstimate(flops=4 * near.size, bytes_accessed=8 * near.size, transcendentals=0),
        name="relay_sum",
    )(near_recv, near, far, *arrived)


def axes_size(axes):
    size = 1
    for axis in axes:
        size *= lax.axis_size(axis)
    return size


def to_chips(array, axes):
    chips = axes_size(axes)
    rows, width = array.shape
    return lax.all_to_all(array.reshape(chips, rows // chips, width), axes, 0, 0, tiled=False)


def from_chips(spread, axes):
    return lax.all_to_all(spread, axes, 0, 0, tiled=False).reshape(-1, spread.shape[2])


def chip_sum_kernel(split_ref, *rest):
    out_ref = rest[-1]
    total = jnp.sum(split_ref[...].astype(F32), axis=0).astype(BF)
    out_ref[...] = jnp.broadcast_to(total[None], out_ref.shape)


def chip_sum(split, *arrived):
    return pl.pallas_call(
        chip_sum_kernel,
        in_specs=[whole(split)] + [ANY] * len(arrived),
        out_shape=shape(split.shape),
        compiler_params=LIMIT,
        cost_estimate=pl.CostEstimate(flops=split.size, bytes_accessed=4 * split.size, transcendentals=0),
        name="chip_sum",
    )(split, *arrived)


def mid_kernel(core_ref, mu_ref, x_ref, x0, x1, x2, x3, gy_ref, g0, g1, g2, g3, k0, k1, k2, k3, za_ref, zb_ref, wu_ref, vu_ref, wd_ref, ud_ref,
               own_ref, s0, s1, s2, s3, mine_ref, other_ref, hid_ref, gp_ref, wu6, wd6, wdm6):
    step, steps = pl.program_id(0), pl.num_programs(0)

    @pl.when(step == 0)
    def _():
        wu6[0:128, :] = wu_ref[0]
        wd6[:, 0:128] = wd_ref[0]
        wdm6[:, 0:128] = wd_ref[0]
        for k, mask_rows in enumerate((k0, k1, k2, k3)):
            lo = 128 * (k + 1)
            wu6[lo:lo + 128, :] = (wu_ref[k + 1].astype(F32) * mu_ref[k]).astype(BF)
            wd6[:, lo:lo + 128] = wd_ref[k + 1]
            wdm6[:, lo:lo + 128] = (wd_ref[k + 1].astype(F32) * mask_rows[k:k + 1, :].astype(F32)).astype(BF)
        wu6[640:768, :] = vu_ref[...]
        wd6[:, 640:768] = ud_ref[...]
        wdm6[:, 640:768] = ud_ref[...]

    half = (2 * step) // steps
    z = jnp.where(half == core_ref[0], za_ref[...], zb_ref[...])
    x6 = jnp.concatenate([r[...] for r in (x_ref, x0, x1, x2, x3)] + [z[:, 0:128]], axis=1)
    gy6 = jnp.concatenate([r[...] for r in (gy_ref, g0, g1, g2, g3)] + [z[:, 128:256]], axis=1)
    pre = matmul(x6, wu6[...])
    square = pre * pre
    tanh = jnp.tanh(GELU_C * pre * (1.0 + GELU_A * square))
    cdf = 0.5 * (1.0 + tanh)
    hidden = (pre * cdf).astype(BF)
    hid_ref[...] = hidden
    slope = cdf + (0.5 * GELU_C) * pre * (1.0 - tanh * tanh) * (1.0 + (3.0 * GELU_A) * square)
    grad_hid = matmul_nt(gy6, wdm6[...])
    grad_pre = (grad_hid * slope).astype(BF)
    gp_ref[...] = grad_pre
    down = matmul(hidden, wd6[...])
    back = matmul_nt(grad_pre, wu6[...])
    own_ref[:, 0:128] = down[:, 0:128]
    own_ref[:, 128:256] = back[:, 0:128]
    for k, send in enumerate((s0, s1, s2, s3)):
        lo = 128 * (k + 1)
        send[:, 0:128] = down[:, lo:lo + 128].astype(BF)
        send[:, 128:256] = back[:, lo:lo + 128].astype(BF)
    part = jnp.concatenate([down[:, 640:768], back[:, 640:768]], axis=1).astype(BF)

    @pl.when(half == core_ref[0])
    def _():
        mine_ref[...] = part

    @pl.when(half != core_ref[0])
    def _():
        other_ref[...] = part


def weights_kernel(mu_ref, core_ref, x_ref, x0, x1, x2, x3, gy_ref, g0, g1, g2, g3, k0, k1, k2, k3, za_ref, zb_ref,
                   hid_ref, gp_ref, *rest):
    gwd_ref, gwu_ref, acc_d, acc_u = rest[-4:]
    step, steps = pl.program_id(0), pl.num_programs(0)

    @pl.when(step == 0)
    def _():
        acc_d[...] = jnp.zeros_like(acc_d)
        acc_u[...] = jnp.zeros_like(acc_u)

    z = jnp.where((2 * step) // steps == core_ref[0], za_ref[...], zb_ref[...])
    x6 = jnp.concatenate([r[...] for r in (x_ref, x0, x1, x2, x3)] + [z[:, 0:128]], axis=1)
    gy6 = jnp.concatenate([r[...] for r in (gy_ref, g0, g1, g2, g3)] + [z[:, 128:256]], axis=1)
    acc_d[...] += matmul_tn(hid_ref[...], gy6)
    acc_u[...] += matmul_tn(x6, gp_ref[...])

    @pl.when(step == steps - 1)
    def _():
        for k in range(6):
            lo = 128 * k
            g_down = acc_d[:, lo:lo + 128]
            g_up = acc_u[lo:lo + 128, :]
            if 1 <= k <= 4:
                g_down = g_down * (k0, k1, k2, k3)[k - 1][k - 1:k, :].astype(F32)
                g_up = g_up * mu_ref[k - 1]
            gwd_ref[k] = g_down.astype(BF)
            gwu_ref[k] = g_up.astype(BF)


def weights(mu, core, x, gy, xs, gys, za, zb, hidden, grad_pre, *arrived):
    tokens, hg = hidden.shape
    steps = tokens // TILE
    thin = pl.BlockSpec((TILE, 128), lambda i: (i, 0))
    wide = pl.BlockSpec((TILE, hg), lambda i: (i, 0))
    z_row = pl.BlockSpec((TILE, 256), lambda i: (lax.rem(i, steps // 2), 0))
    mask_rows = pl.BlockSpec((PAD, 128), lambda i: (tokens // PAD, 0))
    grads = [shape((6, hg, 128)), shape((6, 128, hg))]
    return pl.pallas_call(
        weights_kernel,
        grid=(steps,),
        in_specs=[SMEM, SMEM] + [thin] * 10 + [mask_rows] * 4 + [z_row] * 2 + [wide] * 2 + [ANY] * len(arrived),
        out_specs=[whole(g) for g in grads],
        out_shape=grads,
        scratch_shapes=[pltpu.VMEM((hg, 768), F32), pltpu.VMEM((768, hg), F32)],
        compiler_params=pltpu.CompilerParams(vmem_limit_bytes=56 * 2**20),
        cost_estimate=pl.CostEstimate(flops=4 * tokens * hg * 768, bytes_accessed=14 * 2**20, transcendentals=0),
        name="weights",
    )(mu, core, x, *xs, gy, *gys, *gys, za, zb, hidden, grad_pre, *arrived)


def mid(mu, core, x, gy, xs, gys, za, zb, w_up, v_up, w_down, u_down):
    tokens = 2 * za.shape[0]
    hg = w_up.shape[2]
    steps = tokens // TILE
    half = steps // 2
    row = pl.BlockSpec((TILE, 256), lambda i, c: (i, 0))
    thin = pl.BlockSpec((TILE, 128), lambda i, c: (i, 0))
    wide = pl.BlockSpec((TILE, hg), lambda i, c: (i, 0))
    z_row = pl.BlockSpec((TILE, 256), lambda i, c: (lax.rem(i, half), 0))
    first_rows = lambda i: jnp.minimum(i, half - 1)
    second_rows = lambda i: jnp.maximum(i - half, 0)
    mine = pl.BlockSpec((TILE, 256), lambda i, c: (jnp.where(c[0] == 0, first_rows(i), second_rows(i)), 0))
    other = pl.BlockSpec((TILE, 256), lambda i, c: (jnp.where(c[0] == 0, second_rows(i), first_rows(i)), 0))
    mask_rows = pl.BlockSpec((PAD, 128), lambda i, c: (tokens // PAD, 0))
    return pl.pallas_call(
        mid_kernel,
        grid_spec=pltpu.PrefetchScalarGridSpec(
            num_scalar_prefetch=1,
            grid=(steps,),
            in_specs=[SMEM] + [thin] * 10 + [mask_rows] * 4 + [z_row] * 2
            + [whole(w_up), whole(v_up), whole(w_down), whole(u_down)],
            out_specs=[row] * 5 + [mine, other] + [wide] * 2,
            scratch_shapes=[pltpu.VMEM((768, hg), BF), pltpu.VMEM((hg, 768), BF), pltpu.VMEM((hg, 768), BF)],
        ),
        out_shape=[shape((tokens, 256), F32)] + [shape((tokens, 256))] * 4 + [shape((tokens // 2, 256))] * 2
        + [shape((tokens, hg))] * 2,
        compiler_params=pltpu.CompilerParams(vmem_limit_bytes=56 * 2**20),
        cost_estimate=pl.CostEstimate(
            flops=8 * tokens * hg * 768, bytes_accessed=20 * 2**20, transcendentals=tokens * hg),
        name="mid",
    )(core, mu, x, *xs, gy, *gys, *gys, za, zb, w_up, v_up, w_down, u_down)


def grad_kernel(a_ref, b_ref, five_ref, one_ref):
    total = a_ref[...].astype(F32) + b_ref[...].astype(F32)
    five_ref[...] = total[0:5]
    one_ref[...] = total[5]


def grad_sum(a, b):
    dims = a.shape[1:]
    return pl.pallas_call(
        grad_kernel,
        in_specs=[whole(a), whole(b)],
        out_shape=[shape((5,) + dims, F32), shape(dims, F32)],
        compiler_params=LIMIT,
        cost_estimate=pl.CostEstimate(flops=a.size, bytes_accessed=8 * a.size, transcendentals=0),
        name="grad_sum",
    )(a, b)


def low_kernel(core_ref, x_ref, gy_ref, za_ref, zb_ref, *rest):
    out_ref = rest[-1]
    first_half = core_ref[0] == 0
    half = za_ref.shape[0]
    za, zb = za_ref[...], zb_ref[...]
    z0, z1 = jnp.where(first_half, za, zb), jnp.where(first_half, zb, za)
    out_ref[0] = (matmul_tn(z0[:, 0:128], gy_ref[0:half]) + matmul_tn(z1[:, 0:128], gy_ref[half:])).astype(BF)
    out_ref[1] = (matmul_tn(x_ref[0:half], z0[:, 128:256]) + matmul_tn(x_ref[half:], z1[:, 128:256])).astype(BF)


def low_grads(core, x, gy, za, zb, *arrived):
    return pl.pallas_call(
        low_kernel,
        in_specs=[SMEM, whole(x), whole(gy), whole(za), whole(zb)] + [ANY] * len(arrived),
        out_shape=shape((2, 128, 128)),
        compiler_params=LIMIT,
        cost_estimate=pl.CostEstimate(flops=4 * x.size * 128, bytes_accessed=4 * x.size, transcendentals=0),
        name="low_grads",
    )(core, x, gy, za, zb, *arrived)


def last_kernel(md_ref, core_ref, own_ref, b0, b1, b3, za_ref, zb_ref, vd_ref, uu_ref, out_ref, gx_ref):
    step, steps = pl.program_id(0), pl.num_programs(0)
    z = jnp.where((2 * step) // steps == core_ref[0], za_ref[...], zb_ref[...])
    out = own_ref[:, 0:128] + matmul(z[:, 0:128], vd_ref[...])
    out = out + md_ref[0] * b0[:, 0:128].astype(F32) + md_ref[3] * b3[:, 0:128].astype(F32)
    out_ref[...] = (out + b1[:, 0:128].astype(F32)).astype(BF)
    gx = own_ref[:, 128:256] + matmul_nt(z[:, 128:256], uu_ref[...])
    gx = gx + b0[:, 128:256].astype(F32) + b3[:, 128:256].astype(F32)
    gx_ref[...] = (gx + b1[:, 128:256].astype(F32)).astype(BF)


def last(md, core, own, b0, b1, b3, za, zb, v_down, u_up):
    tokens = own.shape[0]
    steps = tokens // LAST_TILE
    row = pl.BlockSpec((LAST_TILE, 256), lambda i: (i, 0))
    z_row = pl.BlockSpec((LAST_TILE, 256), lambda i: (lax.rem(i, steps // 2), 0))
    out = pl.BlockSpec((LAST_TILE, 128), lambda i: (i, 0))
    return pl.pallas_call(
        last_kernel,
        grid=(steps,),
        in_specs=[SMEM, SMEM] + [row] * 4 + [z_row] * 2 + [whole(v_down), whole(u_up)],
        out_specs=[out, out],
        out_shape=[shape((tokens, 128))] * 2,
        compiler_params=LIMIT,
        cost_estimate=pl.CostEstimate(flops=4 * tokens * 128 * 128, bytes_accessed=7 * 2**20, transcendentals=0),
        name="last",
    )(md, core, own, b0, b1, b3, za, zb, v_down, u_up)


def per_device(activations, w_up, w_down, u_up, v_up, u_down, v_down, mask_up, mask_down, grad_y):
    mu = mask_up[:, 0].astype(F32)
    md = mask_down[:, 0].astype(F32)
    core = lax.axis_index("c").reshape(1)
    x0 = swapped(activations, "c", 1)
    x1 = swapped(activations, "z", 1)
    x3 = swapped(activations, "xl", 1)
    x2 = swapped(x1, "z", 3)
    gym, mine, other = first(core, md, activations, grad_y, u_up, v_down)
    split = to_chips(pair_sum(mine, swapped(other, "c", 1)), CHIPS)
    gym = gate(gym, x1, x3)
    g0 = swapped(gym, "c", 1)
    g1 = swapped(gym, "z", 1)
    g3 = swapped(gym, "xl", 1)
    g2 = swapped(g1, "z", 3)
    za = from_chips(chip_sum(split, x2, g3), CHIPS)
    zb = swapped(za, "c", 1)
    own, s0, s1, s2, s3, mine, other, hidden, grad_pre = mid(
        mu, core, activations, grad_y, (x0, x1, x2, x3), (g0, g1, g2, g3), za, zb, w_up, v_up, w_down, u_down)
    b3 = swapped(s3, "xl", 1)
    b0 = swapped(s0, "c", 1)
    gwd, gwu = weights(
        mu, core, activations, grad_y, (x0, x1, x2, x3), (g0, g1, g2, g3), za, zb, hidden, grad_pre)
    total, s2 = board_sum(to_chips(pair_sum(mine, swapped(other, "c", 1)), BOARD), s2, gwd)
    total_other = swapped(total, "xl", 1)
    far = swapped(s2, "z", 3)
    gwd_other = swapped(gwd, "dp", 1)
    gwu_other = swapped(gwu, "dp", 1)
    spread = spread_sum(total, total_other, b3)
    za = from_chips(spread, BOARD)
    near = relay_sum(g1, s1, far)
    b1 = swapped(near, "z", 1)
    zb = swapped(za, "c", 1)
    low = low_grads(core, activations, grad_y, za, zb)
    low_other = swapped(low, "dp", 1)
    out, grad_x = last(md, core, own, b0, b1, b3, za, zb, v_down, u_up)
    g_down, g_u_down = grad_sum(gwd, gwd_other)
    g_up, g_v_up = grad_sum(gwu, gwu_other)
    g_low = low.astype(F32) + low_other.astype(F32)
    return (out, grad_x, g_up, g_down, g_low[1], g_v_up, g_u_down, g_low[0])


def solution(mesh):
    fine = jax.sharding.Mesh(mesh.devices.reshape(2, 4, 2, 4, 2), ("dp", "y", "xl", "z", "c"))
    mp = ("y", "xl", "z", "c")
    tok = P("dp", mp)
    rows, cols = P(mp, None), P(None, mp)
    up3, down3 = P(None, None, mp), P(None, mp, None)
    return jax.shard_map(
        per_device,
        mesh=fine,
        in_specs=(tok, up3, down3, rows, cols, rows, cols, cols, cols, tok),
        out_specs=(tok, tok, up3, down3, rows, cols, rows, cols),
        check_vma=False,
    )
```
